128 devices in a mesh: rep: 64 (over z_lo, y, x, core), grp: 2 (over z_hi).
Axes of the slice: x: 4, y: 4, z: 4 (z_hi: 2, z_lo: 2; z = z_hi * 2 + z_lo), core: 2. Of those that a mesh axis runs over, the one named last changes fastest.
Arguments:
- tokens: bfloat16 [32768, 1024], P(('rep', 'grp')), may hold values from -6 to 6
- segments: int32 [32768], P(('rep', 'grp')), may hold values from 1 to 10, as said below
- in_gain: bfloat16 [1024], P('grp'), may hold values from 0.5 to 1.5
- w_in: bfloat16 [1024, 4384], P('grp'), may hold values from -0.1875 to 0.1875
- conv_w: bfloat16 [4, 2304], P(None, 'grp'), may hold values from -3 to 3
- conv_b: bfloat16 [2304], P('grp'), may hold values from -1.5 to 1.5
- dt_bias: bfloat16 [32], P('grp'), may hold values from -6 to -1
- a_log: bfloat16 [32], P('grp'), may hold values from 0 to 2.765625
- d_skip: bfloat16 [32], P('grp'), may hold values from 0.5 to 1.5
- gate_gain: bfloat16 [2048], P('grp'), may hold values from 0.5 to 1.5
- w_out: bfloat16 [2048, 1024], P('grp'), may hold values from -0.125 to 0.125
- cotangent: bfloat16 [32768, 1024], P(('rep', 'grp')), may hold values from -6 to 6
Outputs:
- mixed: bfloat16 [32768, 1024], P(('rep', 'grp'))
- input_grad: float32 [32768, 1024], P(('rep', 'grp'))
- in_gain_grad: float32 [1024], P('grp')
- w_in_grad: float32 [1024, 4384], P('grp')
- conv_w_grad: float32 [4, 2304], P(None, 'grp')
- conv_b_grad: float32 [2304], P('grp')
- dt_bias_grad: float32 [32], P('grp')
- a_log_grad: float32 [32], P('grp')
- d_skip_grad: float32 [32], P('grp')
- gate_gain_grad: float32 [2048], P('grp')
- w_out_grad: float32 [2048, 1024], P('grp')
The draws below stay inside these ranges and needn't reach their ends.
Inputs may be any that keep to these rules, and one draw needn't show every extreme that they name: `segments`: within each sequence of 512 tokens the numbers start at 1, never fall and rise by one at each new document; documents hold 60 to 800 tokens except where a sequence's start or end cuts them; one document of each sequence holds both tokens 256 - 1 and 256 of it, and in the first sequence that document holds exactly min(800, 512) tokens.
All inputs are finite; a program needn't handle non-finite values.
Results may differ from the reference program's by a relative error of at most 0.0069.
Values may be sent and summed in bfloat16 or wider, within the bound.
A program may use at most 192 MiB of HBM per device.

```python
import jax
import jax.numpy as jnp
from jax import lax

D = 1024
HEADS = 32
HEAD_DIM = 64
STATE = 128
CONV = 4
STRETCH = 256
INNER = 2048
XBC = 2304
PROJ = 4384
TOK_DEV = 256
DOC_MIN = 60
DOC_MAX = 800
SEQ_LEN = 512
TOKENS = 32768
N_REP = 64


def one_sequence(key, index):
    first, second, third, fourth = jax.random.split(key, 4)
    longest = min(DOC_MAX, SEQ_LEN)
    drawn = jax.random.randint(first, (), DOC_MIN, longest + 1)
    span = jnp.where(index == 0, longest, drawn).astype(jnp.int32)
    low_start = jnp.maximum(0, TOK_DEV - span + 1)
    high_start = jnp.minimum(TOK_DEV - 1, SEQ_LEN - span)
    start = jax.random.randint(second, (), low_start, high_start + 1)
    many = SEQ_LEN // DOC_MIN + 1
    left = start - jnp.cumsum(jax.random.randint(third, (many,), DOC_MIN, DOC_MAX + 1))
    right_lengths = jax.random.randint(fourth, (many,), DOC_MIN, DOC_MAX + 1)
    right = start + span + jnp.cumsum(jnp.concatenate([jnp.zeros((1,), jnp.int32), right_lengths]))
    cuts = jnp.concatenate([left, start[None], right])
    valid = (cuts > 0) & (cuts < SEQ_LEN)
    places = jnp.arange(SEQ_LEN)
    counted = (cuts[None, :] <= places[:, None]) & valid[None, :]
    random_ids = 1 + jnp.sum(counted.astype(jnp.int32), axis=1)
    packed_ids = jnp.where(places >= 1, (places - 1) // DOC_MIN + 2, 1)
    return jnp.where(index == 1, packed_ids, random_ids).astype(jnp.int32)


def draw_segments(key, part):
    key = jax.random.fold_in(key, 7)
    keys = jax.random.split(key, TOKENS // SEQ_LEN)
    order = jnp.arange(TOKENS // SEQ_LEN, dtype=jnp.int32)
    return jax.vmap(one_sequence)(keys, order).reshape(TOKENS).astype(jnp.int32)


def shard_levels(key, shape, shards, least, high):
    level, own = 1.0, jax.random.fold_in(key, 6)
    for dim, blocks in shards:
        steps = jnp.exp(jax.random.uniform(jax.random.fold_in(own, dim), (blocks,), jnp.float32, least / len(shards), high / len(shards)))
        level = level * jnp.repeat(steps, shape[dim] // blocks).reshape([-1 if axis == dim else 1 for axis in range(len(shape))])
    return level


def gaussian(stream_key, dims, scale, bound, cuts=(), held_as=jnp.bfloat16):
    level = shard_levels(stream_key, dims, cuts, -0.22, 0.18) if cuts else 1.0
    values = jax.random.normal(stream_key, dims, jnp.float32) * scale * level
    return jnp.minimum(jnp.maximum(values, -bound), bound).astype(held_as)


def setup_inputs(seed: int = 0) -> dict:
    streams_of = jax.random.split(jax.random.key(seed), 13)
    tokens = gaussian(streams_of[0], (TOKENS, D), 1.0, 6.0, ((0, 128),))
    segments = draw_segments(jax.random.fold_in(streams_of[12], 71), 0)
    in_gain = jnp.clip(1.0 + 0.1 * jax.random.normal(streams_of[2], (D,), jnp.float32), 0.5, 1.5).astype(jnp.bfloat16)
    w_in = gaussian(streams_of[3], (D, PROJ), D ** -0.5, 0.1875, ((0, 2),))
    conv_w = gaussian(streams_of[4], (CONV, XBC), CONV ** -0.5, 3.0, ((1, 2),))
    conv_b = gaussian(streams_of[5], (XBC,), 0.3, 1.5, ((0, 2),))
    dt_bias = jnp.clip(-6.0 + 5.0 * jax.random.uniform(streams_of[6], (HEADS,), jnp.float32) ** shard_levels(streams_of[6], (HEADS,), ((0, 2),), -0.2, 0.2), -6.0, -1.0).astype(jnp.bfloat16)
    a_log = jnp.clip(2.765625 * jax.random.uniform(streams_of[7], (HEADS,), jnp.float32) ** shard_levels(streams_of[7], (HEADS,), ((0, 2),), -0.2, 0.2), 0.0, 2.765625).astype(jnp.bfloat16)
    d_skip = jnp.clip(0.5 + 1.0 * jax.random.uniform(streams_of[8], (HEADS,), jnp.float32) ** shard_levels(streams_of[8], (HEADS,), ((0, 2),), -0.2, 0.2), 0.5, 1.5).astype(jnp.bfloat16)
    gate_gain = jnp.clip(1.0 + 0.1 * jax.random.normal(streams_of[9], (INNER,), jnp.float32), 0.5, 1.5).astype(jnp.bfloat16)
    w_out = gaussian(streams_of[10], (INNER, D), INNER ** -0.5, 0.125, ((0, 2),))
    cotangent = gaussian(streams_of[11], (TOKENS, D), 1.0, 6.0, ((0, 128),))
    return dict(tokens=tokens, segments=segments, in_gain=in_gain, w_in=w_in, conv_w=conv_w, conv_b=conv_b, dt_bias=dt_bias, a_log=a_log, d_skip=d_skip, gate_gain=gate_gain, w_out=w_out, cotangent=cotangent)


EPS = 1e-05
HIGHEST = lax.Precision.HIGHEST

@jax.custom_vjp
def low(v):
    return lax.optimization_barrier(v.astype(jnp.bfloat16)).astype(jnp.float32)

@jax.custom_vjp
def low_back(v):
    return v

def low_keep(v):
    return (low(v), None)

def low_pass(kept, grad):
    return (grad,)

def back_keep(v):
    return (v, None)

def back_low(kept, grad):
    return (low(grad),)
low.defvjp(low_keep, low_pass)
low_back.defvjp(back_keep, back_low)

def prenorm(inputs, gain):
    square = lax.optimization_barrier(jnp.mean(inputs * inputs, axis=1, keepdims=True))
    return inputs * lax.rsqrt(square + EPS) * gain[None, :]

def mix_inputs(extended, ext_seg, seg_ids, dt_raw, conv_weight, conv_bias, dt_bias, a_log):
    count = seg_ids.shape[0]
    total = jnp.zeros((count, extended.shape[1]), jnp.float32) + conv_bias[None, :]
    for offset in range(CONV):
        rows = extended[offset:offset + count]
        same = (ext_seg[offset:offset + count] == seg_ids).astype(jnp.float32)
        total = total + conv_weight[offset][None, :] * rows * same[:, None]
    active = jax.nn.silu(total)
    head_in = active[:, :INNER].reshape(count, HEADS, HEAD_DIM)
    b_mat = active[:, INNER:INNER + STATE]
    c_mat = active[:, INNER + STATE:]
    step_size = jax.nn.softplus(dt_raw + dt_bias[None, :])
    decay_rate = -jnp.exp(a_log)
    return (head_in, b_mat, c_mat, step_size, decay_rate)

def ssd_block(head_in, b_mat, c_mat, step_size, decay_rate, state, seg_ids, prev_seg):
    log_decay = step_size * decay_rate[None, :]
    running = jnp.cumsum(log_decay, axis=0)
    length = seg_ids.shape[0]
    places = jnp.arange(length)
    allowed = (places[:, None] >= places[None, :]) & (seg_ids[:, None] == seg_ids[None, :])
    spread = running[:, None, :] - running[None, :, :]
    kernel = jnp.where(allowed[:, :, None], jnp.exp(jnp.where(allowed[:, :, None], spread, 0.0)), 0.0)
    scores = jnp.dot(c_mat, b_mat.T, precision=HIGHEST)
    weights = kernel * scores[:, :, None] * step_size[None, :, :]
    output = jnp.einsum('tsh,shd->thd', weights, head_in, precision=HIGHEST)
    carried = (seg_ids == prev_seg).astype(jnp.float32)
    enter = jnp.exp(running) * carried[:, None]
    output = output + jnp.einsum('tn,hdn->thd', c_mat, state, precision=HIGHEST) * enter[:, :, None]
    tail = jnp.exp(running[-1][None, :] - running) * (seg_ids == seg_ids[-1]).astype(jnp.float32)[:, None]
    new_state = jnp.einsum('shd,sn->hdn', head_in * (step_size * tail)[:, :, None], b_mat, precision=HIGHEST)
    new_state = new_state + enter[-1][:, None, None] * state
    return (output, new_state, enter)

def gated(ssd_out, head_in, gate_in, skip_weight, norm_gain):
    count = ssd_out.shape[0]
    full = (ssd_out + skip_weight[None, :, None] * head_in).reshape(count, INNER)
    gated_val = full * jax.nn.silu(gate_in)
    square = lax.optimization_barrier(jnp.mean(gated_val * gated_val, axis=1, keepdims=True))
    return gated_val * lax.rsqrt(square + EPS) * norm_gain[None, :]

def layer(inputs, seg_ids, in_gain, w_in, conv_w, conv_b, dt_bias, a_log, d_skip, gate_gain, w_out):
    normed = low(prenorm(inputs, in_gain))
    proj = low_back(jnp.dot(normed, w_in, precision=HIGHEST))
    gate_in = proj[:, :INNER]
    conv_in = proj[:, INNER:INNER + INNER + 2 * STATE]
    dt_raw = proj[:, INNER + INNER + 2 * STATE:]
    extended = jnp.concatenate([jnp.zeros((CONV - 1, conv_in.shape[1]), jnp.float32), conv_in], axis=0)
    ext_seg = jnp.concatenate([jnp.zeros((CONV - 1,), jnp.int32), seg_ids]).astype(jnp.int32)
    head_in, b_mat, c_mat, step_size, decay_rate = mix_inputs(extended, ext_seg, seg_ids, dt_raw, conv_w, conv_b, dt_bias, a_log)
    width = min(STRETCH, TOK_DEV)
    blocks = SEQ_LEN // width
    seg_blocks = seg_ids.reshape(blocks, width)
    prev_blocks = jnp.concatenate([jnp.zeros((1,), jnp.int32), seg_blocks[:-1, -1]]).astype(jnp.int32)

    def advance(state, pieces):
        head_part, b_part, c_part, step_part, seg_part, prev_part = pieces
        output, new_state, enter = ssd_block(head_part, b_part, c_part, step_part, decay_rate, state, seg_part, prev_part)
        return (new_state, output)
    _, ssd_out = lax.scan(jax.checkpoint(advance), jnp.zeros((HEADS, HEAD_DIM, STATE), jnp.float32), (head_in.reshape(blocks, width, HEADS, HEAD_DIM), b_mat.reshape(blocks, width, STATE), c_mat.reshape(blocks, width, STATE), step_size.reshape(blocks, width, HEADS), seg_blocks, prev_blocks))
    ssd_out = ssd_out.reshape(SEQ_LEN, HEADS, HEAD_DIM)
    branch = low(gated(ssd_out, head_in, gate_in, d_skip, gate_gain))
    return inputs + jnp.dot(branch, w_out, precision=HIGHEST)

def reference(tokens, segments, in_gain, w_in, conv_w, conv_b, dt_bias, a_log, d_skip, gate_gain, w_out, cotangent):
    weights = tuple((item.astype(jnp.float32) for item in (in_gain, w_in, conv_w, conv_b, dt_bias, a_log, d_skip, gate_gain, w_out)))
    seqs_in = tokens.astype(jnp.float32).reshape(N_REP, SEQ_LEN, D)
    seqs_seg = segments.reshape(N_REP, SEQ_LEN)
    seqs_grad = cotangent.astype(jnp.float32).reshape(N_REP, SEQ_LEN, D)

    def one(totals, item):
        seq_in, seq_seg, seq_grad = item

        def apply(inputs, *params):
            return layer(inputs, seq_seg, *params)
        output, pull = jax.vjp(apply, seq_in, *weights)
        grads = pull(seq_grad)
        totals = tuple((left + right for left, right in zip(totals, grads[1:])))
        return (totals, (output.astype(jnp.bfloat16), grads[0]))
    start = tuple((jnp.zeros(item.shape, jnp.float32) for item in weights))
    totals, (outputs, input_grads) = lax.scan(one, start, (seqs_in, seqs_seg, seqs_grad))
    mixed = outputs.reshape(TOKENS, D)
    input_grad = input_grads.reshape(TOKENS, D)
    return (mixed, input_grad, totals[0], totals[1], totals[2], totals[3], totals[4], totals[5], totals[6], totals[7], totals[8])
```

```python
import jax
import jax.numpy as jnp
from jax import lax
from jax.experimental import pallas as pl
from jax.experimental.pallas import tpu as pltpu
from jax.sharding import PartitionSpec as P

HEADS = 32
HEAD_DIM = 64
STATE = 128
CONV = 4
STRETCH = 256
INNER = 2048


EPS = 1e-05
HIGHEST = lax.Precision.HIGHEST


def from_behind(block, axis, distance):
    devices = range(lax.axis_size(axis))
    route = [(i - distance, i) for i in devices if i - distance in devices]
    return lax.ppermute(block, axis, route)


def entering(shard, axis, combine, identity):
    length, here = (lax.axis_size(axis), lax.axis_index(axis))
    everything = jax.tree.map(lambda part: lax.all_gather(part, axis), shard)
    start = jax.tree.map(
        lambda part, zero: jnp.broadcast_to(jnp.asarray(zero, part.dtype), part.shape),
        shard,
        identity,
    )

    def entering_step(k, before):
        reached = k < here
        new = combine(before, jax.tree.map(lambda part: part[k], everything))
        return jax.tree.map(lambda a, b: jnp.where(reached, a, b), new, before)

    return lax.fori_loop(0, length, entering_step, start)


def prefix(shard, axis, combine, identity):
    length, here = (lax.axis_size(axis), lax.axis_index(axis))
    everything = jax.tree.map(
        lambda part, kind: lax.all_gather(part.astype(kind), axis),
        shard,
        jax.tree.map(lambda a: jnp.bfloat16 if a.dtype == jnp.float32 else a.dtype, shard),
    )
    start = jax.tree.map(
        lambda part, zero: jnp.broadcast_to(jnp.asarray(zero, part.dtype), part.shape),
        shard,
        identity,
    )

    def prefix_step(k, before):
        at = length - 1 - k
        reached = at > here
        new = combine(
            before, jax.tree.map(lambda part, own: part[at].astype(own.dtype), everything, shard)
        )
        return jax.tree.map(lambda a, b: jnp.where(reached, a, b), new, before)

    return lax.fori_loop(0, length, prefix_step, start)


def prenorm(inputs, gain):
    square = jnp.mean(inputs * inputs, axis=1, keepdims=True)
    return inputs * lax.rsqrt(square + EPS) * gain[None, :]


def mix_inputs(extended, ext_seg, seg_ids, dt_raw, conv_weight, conv_bias, dt_bias, a_log):
    count = seg_ids.shape[0]
    total = jnp.zeros((count, extended.shape[1]), jnp.float32) + conv_bias[None, :]
    for offset in range(CONV):
        rows = extended[offset : offset + count]
        same = (ext_seg[offset : offset + count] == seg_ids).astype(jnp.float32)
        total = total + conv_weight[offset][None, :] * rows * same[:, None]
    active = jax.nn.silu(total)
    head_in = active[:, :INNER].reshape(count, HEADS, HEAD_DIM)
    b_mat = active[:, INNER : INNER + STATE]
    c_mat = active[:, INNER + STATE :]
    step_size = jax.nn.softplus(dt_raw + dt_bias[None, :])
    decay_rate = -jnp.exp(a_log)
    return (head_in, b_mat, c_mat, step_size, decay_rate)


def ssd_block(head_in, b_mat, c_mat, step_size, decay_rate, state, seg_ids, prev_seg):
    log_decay = step_size * decay_rate[None, :]
    running = jnp.cumsum(log_decay, axis=0)
    length = seg_ids.shape[0]
    places = jnp.arange(length)
    allowed = (places[:, None] >= places[None, :]) & (seg_ids[:, None] == seg_ids[None, :])
    spread = running[:, None, :] - running[None, :, :]
    kernel = jnp.where(
        allowed[:, :, None], jnp.exp(jnp.where(allowed[:, :, None], spread, 0.0)), 0.0
    )
    scores = jnp.dot(c_mat, b_mat.T, precision=HIGHEST)
    weights = kernel * scores[:, :, None] * step_size[None, :, :]
    output = jnp.einsum("tsh,shd->thd", weights, head_in, precision=HIGHEST)
    carried = (seg_ids == prev_seg).astype(jnp.float32)
    enter = jnp.exp(running) * carried[:, None]
    output = output + jnp.einsum("tn,hdn->thd", c_mat, state, precision=HIGHEST) * enter[:, :, None]
    tail = (
        jnp.exp(running[-1][None, :] - running)
        * (seg_ids == seg_ids[-1]).astype(jnp.float32)[:, None]
    )
    new_state = jnp.einsum(
        "shd,sn->hdn", head_in * (step_size * tail)[:, :, None], b_mat, precision=HIGHEST
    )
    new_state = new_state + enter[-1][:, None, None] * state
    return (output, new_state, enter)


def gated(ssd_out, head_in, gate_in, skip_weight, norm_gain):
    count = ssd_out.shape[0]
    full = (ssd_out + skip_weight[None, :, None] * head_in).reshape(count, INNER)
    gated_val = full * jax.nn.silu(gate_in)
    square = jnp.mean(gated_val * gated_val, axis=1, keepdims=True)
    return gated_val * lax.rsqrt(square + EPS) * norm_gain[None, :]


def chain(earlier, later):
    return (earlier[0] * later[0], later[1] + later[0][:, None, None] * earlier[1])


MESH = pl.DeviceIdType.MESH
RIM = 4
LANES = 128
W_IN_COLS = 4608
PARTS = (
    ("x", "y", "z", 0, 1152),
    ("y", "z", "x", 1152, 1152),
    ("z", "x", "y", 2304, 1024),
)
OWN_COLS = 3328
ALL_COLS = 6656
N_SEMS = 128


def place():
    rep, grp = lax.axis_index("rep"), lax.axis_index("grp")
    here = {
        "core": lax.rem(rep, 2),
        "x": lax.rem(lax.div(rep, 2), 4),
        "y": lax.rem(lax.div(rep, 8), 4),
        "z": 2 * grp + lax.div(rep, 32),
    }
    return here


def device_at(here):
    low_z = lax.rem(here["z"], 2)
    rep = ((low_z * 4 + here["y"]) * 4 + here["x"]) * 2 + here["core"]
    return (rep, lax.div(here["z"], 2))


def moved(here, axis, by):
    there = dict(here)
    there[axis] = lax.rem(here[axis] + (by % 4), 4)
    return there


def other_core(here):
    there = dict(here)
    there["core"] = 1 - here["core"]
    return there


def greet(partners):
    barrier = pltpu.get_barrier_semaphore()
    for partner in partners:
        pl.semaphore_signal(barrier, inc=1, device_id=partner, device_id_type=MESH)
    pl.semaphore_wait(barrier, len(partners))


class Copies:
    def __init__(self, send_sems, recv_sems):
        self.send_sems, self.recv_sems = send_sems, recv_sems
        self.made = []

    def start(self, src, dst, device):
        at = len(self.made)
        copy = pltpu.make_async_remote_copy(
            src_ref=src,
            dst_ref=dst,
            send_sem=self.send_sems.at[at],
            recv_sem=self.recv_sems.at[at],
            device_id=device,
            device_id_type=MESH,
        )
        copy.start()
        self.made.append(copy)
        return copy

    def finish(self):
        for copy in self.made:
            copy.wait_send()


def view(ref, axes, cols):
    return ref.at[axes["x"], axes["y"], axes["z"], :, cols]


def halves(axes, free, sizes):
    if not free:
        return (axes, None)
    name = free[0]
    half = sizes[name] // 2
    return (
        dict(axes, **{name: slice(0, half)}),
        dict(axes, **{name: slice(half, 2 * half)}),
    )


def reduce_kernel(
    normed_ref,
    pg_ref,
    branch_ref,
    cot_ref,
    strip_ref,
    out_ref,
    far_normed,
    far_pg,
    far_branch,
    far_cot,
    far_strip,
    buf,
    half_a,
    half_b,
    half_c,
    whole_a,
    whole_b,
    whole_c,
    half_a1,
    half_b1,
    half_c1,
    whole_a1,
    whole_b1,
    whole_c1,
    last_a,
    last_b,
    last_c,
    send_sems,
    recv_sems,
):
    here = place()
    core = here["core"]
    twin = device_at(other_core(here))
    greet(
        [twin]
        + [device_at(moved(here, axis, by)) for axis in ("x", "y", "z") for by in (1, -1)]
    )
    copies = Copies(send_sems, recv_sems)

    theirs = 1 - core
    branch_in = []
    for half in range(2):
        cols = pl.ds(pl.multiple_of(1024 * half + 512 * theirs, 512), 512)
        branch_in.append(
            copies.start(branch_ref.at[:, cols], far_branch.at[:, pl.ds(512 * half, 512)], twin)
        )
    cot_in = copies.start(cot_ref, far_cot, twin)
    normed_in = copies.start(normed_ref, far_normed, twin)
    pg_in = []
    for part in range(2):
        cols = pl.ds(pl.multiple_of(2304 * part + 1152 * theirs, 128), 1152)
        pg_in.append(
            copies.start(pg_ref.at[:, cols], far_pg.at[:, pl.ds(1152 * part, 1152)], twin)
        )
    strip_in = copies.start(strip_ref, far_strip, twin)

    half_in = ((half_a, half_b, half_c), (half_a1, half_b1, half_c1))
    whole_in = ((whole_a, whole_b, whole_c), (whole_a1, whole_b1, whole_c1), (last_a, last_b, last_c))
    sizes = {"x": 4, "y": 4, "z": 4}

    def product(left, right):
        return lax.dot_general(
            left, right, (((0,), (0,)), ((), ())), preferred_element_type=jnp.float32
        )

    def store(row, half, cols, value):
        buf[row, :, 2 * half : 2 * half + 2, :, cols] = value.astype(jnp.bfloat16).reshape(
            4, 2, 16, value.shape[1]
        )

    def stage_axes(part, stage):
        order = PARTS[part][:3]
        axes = {}
        for done in order[:stage]:
            axes[done] = here[done]
        free = [name for name in ("x", "y", "z") if name in order[stage + 1 :]]
        for name in free:
            axes[name] = slice(None)
        return order[stage], axes, free

    live = {}

    def begin(part, stage):
        axis, axes, free = stage_axes(part, stage)
        cols = pl.ds(PARTS[part][3], PARTS[part][4])
        chunk = lambda by: dict(axes, **{axis: lax.rem(here[axis] + (by % 4), 4)})
        ahead, behind = device_at(moved(here, axis, 1)), device_at(moved(here, axis, -1))
        whole = whole_in[stage][part]
        state = {}
        far_first, far_second = halves(chunk(2), free, sizes)
        if stage < 2:
            halved = half_in[stage][part]
            state["a"] = copies.start(view(buf, far_first, cols), halved.at[0], ahead)
            state["b"] = copies.start(view(buf, far_second, cols), halved.at[1], behind)
            low = lambda ref, d: ref.at[d, pl.ds(0, 2)]
            high = lambda ref, d: ref.at[d, pl.ds(2, 2)]
            first, second = halves(chunk(1), free, sizes)
            state["up_free"] = copies.start(view(buf, second, cols), high(whole, 0), ahead)
            first, second = halves(chunk(-1), free, sizes)
            state["down_free"] = copies.start(view(buf, first, cols), low(whole, 1), behind)
        else:
            state["a"] = copies.start(view(buf, far_first, cols), whole.at[2], ahead)
            state["down"] = copies.start(view(buf, chunk(-1), cols), whole.at[1], behind)
        live[part, stage] = state

    def add_into(axes, cols, incoming):
        at = (axes["x"], axes["y"], axes["z"], slice(None), cols)
        total = buf[at].astype(jnp.float32)
        for value in incoming:
            total = total + value.astype(jnp.float32)
        buf[at] = total.astype(jnp.bfloat16)

    def relay(part, stage):
        axis, axes, free = stage_axes(part, stage)
        cols = pl.ds(PARTS[part][3], PARTS[part][4])
        chunk = lambda by: dict(axes, **{axis: lax.rem(here[axis] + (by % 4), 4)})
        ahead, behind = device_at(moved(here, axis, 1)), device_at(moved(here, axis, -1))
        whole = whole_in[stage][part]
        state = live[part, stage]
        state["a"].wait_recv()
        if stage < 2:
            halved = half_in[stage][part]
            first, _ = halves(chunk(1), free, sizes)
            add_into(first, cols, [halved[0]])
            state["up"] = copies.start(view(buf, first, cols), whole.at[0, pl.ds(0, 2)], ahead)
            state["b"].wait_recv()
            _, second = halves(chunk(-1), free, sizes)
            add_into(second, cols, [halved[1]])
            state["down"] = copies.start(view(buf, second, cols), whole.at[1, pl.ds(2, 2)], behind)
        else:
            add_into(chunk(1), cols, [whole[2]])
            state["up"] = copies.start(view(buf, chunk(1), cols), whole.at[0], ahead)

    def settle(part, stage):
        axis, axes, free = stage_axes(part, stage)
        cols = pl.ds(PARTS[part][3], PARTS[part][4])
        whole = whole_in[stage][part]
        state = live[part, stage]
        for name in ("up_free", "down_free", "down", "up"):
            if name in state:
                state[name].wait_recv()
        mine = dict(axes, **{axis: here[axis]})
        if stage < 2:
            add_into(mine, cols, [whole[0], whole[1]])
        else:
            at = (mine["x"], mine["y"], mine["z"], slice(None), cols)
            total = buf[at].astype(jnp.float32)
            total = total + whole[0].astype(jnp.float32) + whole[1].astype(jnp.float32)
            low_z = lax.rem(here["z"], 2)
            out_ref[here["x"], here["y"], low_z, :, out_cols(part)] = total.astype(jnp.bfloat16)

    def out_cols(part):
        start, width = PARTS[part][3:]
        return pl.ds(pl.multiple_of(2 * start + width * core, LANES), width)

    mine = core

    for copy in branch_in:
        copy.wait_recv()
    cot_in.wait_recv()
    for half in range(2):

        @pl.loop(0, 4)
        def _(row):
            near = pl.ds(pl.multiple_of(1024 * half + 512 * mine + 128 * row, 128), 128)
            far = pl.ds(pl.multiple_of(512 * half + 128 * row, 128), 128)
            value = product(branch_ref[:, near], cot_ref[...])
            value = value + product(far_branch[:, far], far_cot[...])
            store(row, half, pl.ds(2304, 1024), value)

    begin(2, 0)
    normed_in.wait_recv()
    strip_in.wait_recv()
    for part in range(2):
        pg_in[part].wait_recv()
        for half in range(2):

            @pl.loop(0, 4)
            def _(row):
                rows = pl.ds(pl.multiple_of(512 * half + 128 * row, 128), 128)
                near = pl.ds(pl.multiple_of(2304 * part + 1152 * mine, 128), 1152)
                value = product(normed_ref[:, rows], pg_ref[:, near])
                value = value + product(
                    far_normed[:, rows], far_pg[:, 1152 * part : 1152 * part + 1152]
                )
                store(row, half, pl.ds(1152 * part, 1152), value)
                if part == 1:
                    small = strip_ref[rows, :].astype(jnp.float32) + far_strip[rows, :].astype(
                        jnp.float32
                    )
                    tail = value[:, 1024:] + small * mine.astype(jnp.float32)
                    store(row, half, pl.ds(2304 - 128, 128), tail)

        begin(part, 0)

    turn = (2, 0, 1)
    for stage in range(3):
        for part in turn:
            relay(part, stage)
        for part in turn:
            settle(part, stage)
            if stage < 2:
                begin(part, stage + 1)

    out_sizes = {"x": 4, "y": 4, "z": 2}
    place_out = {"x": here["x"], "y": here["y"], "z": lax.rem(here["z"], 2)}

    def gather_axes(part, stage):
        order = PARTS[part][:3][::-1]
        axes = {}
        for name in order[stage + 1 :]:
            axes[name] = place_out[name]
        free = [name for name in ("x", "y", "z") if name in order[:stage]]
        for name in free:
            axes[name] = slice(None)
        return order[stage], axes, free

    to_twin = []

    def share(part, stage, axes):
        if stage == 2:
            here_view = view(out_ref, axes, out_cols(part))
            to_twin.append(copies.start(here_view, here_view, twin))

    def spread(part, stage):
        axis, axes, free = gather_axes(part, stage)
        cols = out_cols(part)
        if axis == "z":
            low_z = place_out["z"]
            beside = device_at(dict(here, z=here["z"] + 1 - 2 * low_z))
            piece = view(out_ref, dict(axes, z=low_z), cols)
            live["g", part, stage] = (copies.start(piece, piece, beside),)
            share(part, stage, dict(axes, z=low_z))
            return
        ahead, behind = device_at(moved(here, axis, 1)), device_at(moved(here, axis, -1))
        piece = view(out_ref, dict(axes, **{axis: here[axis]}), cols)
        up = copies.start(piece, piece, ahead)
        down = copies.start(piece, piece, behind)
        live["g", part, stage] = (up, down)
        share(part, stage, dict(axes, **{axis: here[axis]}))

    def forward(part, stage):
        axis, axes, free = gather_axes(part, stage)
        cols = out_cols(part)
        started = live["g", part, stage]
        if axis == "z":
            started[0].wait_recv()
            live["h", part, stage] = ()
            share(part, stage, dict(axes, z=1 - place_out["z"]))
            return
        ahead, behind = device_at(moved(here, axis, 1)), device_at(moved(here, axis, -1))
        before = dict(axes, **{axis: lax.rem(here[axis] + 3, 4)})
        after = dict(axes, **{axis: lax.rem(here[axis] + 1, 4)})
        started[0].wait_recv()
        first, _ = halves(before, free, out_sizes)
        piece = view(out_ref, first, cols)
        more = [copies.start(piece, piece, ahead)]
        share(part, stage, before)
        started[1].wait_recv()
        if free:
            _, second = halves(after, free, out_sizes)
            piece = view(out_ref, second, cols)
            more.append(copies.start(piece, piece, behind))
        share(part, stage, after)
        live["h", part, stage] = tuple(more)

    def complete(part, stage):
        axis, axes, free = gather_axes(part, stage)
        for copy in live["h", part, stage]:
            copy.wait_recv()
        if axis != "z":
            share(part, stage, dict(axes, **{axis: lax.rem(here[axis] + 2, 4)}))

    for stage in range(3):
        for part in turn:
            spread(part, stage)
        for part in turn:
            forward(part, stage)
        for part in turn:
            complete(part, stage)
    for copy in to_twin:
        copy.wait_recv()
    copies.finish()


def reduce_gradients(normed, proj_grad, branch, cotangent, strip):
    bf16 = jnp.bfloat16
    vmem = lambda *shape: pltpu.VMEM(shape, bf16)
    widths = [part[4] for part in PARTS]
    scratch = [
        vmem(256, 1024),
        vmem(256, 2304),
        vmem(256, 1024),
        vmem(256, 1024),
        vmem(1024, 128),
        vmem(4, 4, 4, 16, OWN_COLS),
    ]
    scratch += [vmem(2, 2, 4, 16, width) for width in widths]
    scratch += [vmem(2, 4, 4, 16, width) for width in widths]
    scratch += [vmem(2, 2, 16, width) for width in widths]
    scratch += [vmem(2, 4, 16, width) for width in widths]
    scratch += [vmem(3, 16, width) for width in widths]
    scratch += [pltpu.SemaphoreType.DMA((N_SEMS,)), pltpu.SemaphoreType.DMA((N_SEMS,))]
    out = pl.pallas_call(
        reduce_kernel,
        out_shape=jax.ShapeDtypeStruct((4, 4, 2, 16, ALL_COLS), bf16),
        in_specs=[pl.BlockSpec(memory_space=pltpu.VMEM)] * 5,
        out_specs=pl.BlockSpec(memory_space=pltpu.VMEM),
        scratch_shapes=scratch,
        compiler_params=pltpu.CompilerParams(
            collective_id=0, has_side_effects=True, vmem_limit_bytes=56 * 1024 * 1024
        ),
        name="reduce_gradients",
    )(normed, proj_grad, branch, cotangent, strip)
    return out.reshape(512, ALL_COLS)


def on_device(
    tokens,
    segments,
    in_gain,
    w_in,
    conv_w,
    conv_b,
    dt_bias,
    a_log,
    d_skip,
    gate_gain,
    w_out,
    cotangent,
):
    gathered = (
        lax.all_gather(w_in, "grp", axis=0, tiled=True),
        lax.all_gather(conv_w, "grp", axis=1, tiled=True),
        lax.all_gather(conv_b, "grp", axis=0, tiled=True),
        lax.all_gather(dt_bias, "grp", axis=0, tiled=True),
        lax.all_gather(a_log, "grp", axis=0, tiled=True),
        lax.all_gather(d_skip, "grp", axis=0, tiled=True),
        lax.all_gather(gate_gain, "grp", axis=0, tiled=True),
        lax.all_gather(in_gain, "grp", axis=0, tiled=True),
        lax.all_gather(w_out, "grp", axis=0, tiled=True),
    )
    full_in = gathered[0]
    full_out = gathered[8]
    conv_weight = gathered[1].astype(jnp.float32)
    conv_bias = gathered[2].astype(jnp.float32)
    bias_full = gathered[3].astype(jnp.float32)
    alog_full = gathered[4].astype(jnp.float32)
    skip_full = gathered[5].astype(jnp.float32)
    ggain_full = gathered[6].astype(jnp.float32)
    igain_full = gathered[7].astype(jnp.float32)
    inputs = tokens.astype(jnp.float32)
    count = inputs.shape[0]
    normed, pre_pull = jax.vjp(prenorm, inputs, igain_full)
    normed_low = normed.astype(jnp.bfloat16)
    proj = jnp.dot(normed_low, full_in, preferred_element_type=jnp.float32)
    gate_in = proj[:, :INNER]
    conv_in = proj[:, INNER : INNER + INNER + 2 * STATE]
    dt_raw = proj[:, INNER + INNER + 2 * STATE :]
    rim = CONV - 1
    edge_rows, edge_seg = from_behind(
        (conv_in[count - rim :], segments[count - rim :].astype(jnp.float32)), "grp", 1
    )
    prev_seg = edge_seg.astype(jnp.int32)
    extended = jnp.concatenate([edge_rows, conv_in], axis=0)
    ext_seg = jnp.concatenate([prev_seg, segments])

    def mixing(ext_rows, raw_steps, weight_taps, bias_taps, bias_steps, log_rates):
        return mix_inputs(
            ext_rows, ext_seg, segments, raw_steps, weight_taps, bias_taps, bias_steps, log_rates
        )

    mixed_out, mix_pull = jax.vjp(
        mixing, extended, dt_raw, conv_weight, conv_bias, bias_full, alog_full
    )
    head_in, b_mat, c_mat, step_size, decay_rate = mixed_out
    width = min(STRETCH, count)
    blocks = count // width
    head_blocks = head_in.reshape(blocks, width, HEADS, HEAD_DIM)
    b_blocks = b_mat.reshape(blocks, width, STATE)
    c_blocks = c_mat.reshape(blocks, width, STATE)
    step_blocks = step_size.reshape(blocks, width, HEADS)
    seg_blocks = segments.reshape(blocks, width)
    prev_blocks = jnp.concatenate([prev_seg[rim - 1 :], seg_blocks[:-1, -1]])

    def advance(carry, pieces):
        state, factor = carry
        head_part, b_part, c_part, step_part, seg_part, prev_part = pieces
        output, new_state, enter = ssd_block(
            head_part, b_part, c_part, step_part, decay_rate, state, seg_part, prev_part
        )
        return ((new_state, factor * enter[-1]), (output, state, factor, enter))

    zero_state = jnp.zeros((HEADS, HEAD_DIM, STATE), jnp.float32)
    unit_factor = jnp.ones((HEADS,), jnp.float32)
    (local_state, piece_factor), (partial_value, starts_zero, factors, enters) = lax.scan(
        advance,
        (zero_state, unit_factor),
        (head_blocks, b_blocks, c_blocks, step_blocks, seg_blocks, prev_blocks),
    )
    incoming = entering((piece_factor, local_state), "grp", chain, (unit_factor, zero_state))[1]
    starts = starts_zero + factors[:, :, None, None] * incoming[None]
    weight_in = enters * factors[:, None, :]
    ssd_out = (
        partial_value
        + jnp.einsum("btn,hdn->bthd", c_blocks, incoming, precision=HIGHEST) * weight_in[..., None]
    )
    ssd_out = ssd_out.reshape(count, HEADS, HEAD_DIM)
    branch, gate_pull = jax.vjp(gated, ssd_out, head_in, gate_in, skip_full, ggain_full)
    branch_low = branch.astype(jnp.bfloat16)
    mixed = (inputs + jnp.dot(branch_low, full_out, preferred_element_type=jnp.float32)).astype(
        jnp.bfloat16
    )
    branch_grad = jnp.dot(cotangent, full_out.T, preferred_element_type=jnp.float32)
    ssd_grad, head_gate_grad, gate_in_grad, skip_grad, ggain_grad = gate_pull(branch_grad)
    ssd_grad_blocks = ssd_grad.reshape(blocks, width, HEADS, HEAD_DIM)
    local_grad = jnp.einsum(
        "bth,bthd,btn->hdn", weight_in, ssd_grad_blocks, c_blocks, precision=HIGHEST
    )
    end_grad = prefix((piece_factor, local_grad), "grp", chain, (unit_factor, zero_state))[1]

    def retreat(carry, pieces):
        head_part, b_part, c_part, step_part, seg_part, prev_part, start_part, grad_part = pieces

        def local_block(head_val, b_val, c_val, step_val, rate_val, state_val):
            result = ssd_block(
                head_val, b_val, c_val, step_val, rate_val, state_val, seg_part, prev_part
            )
            return (result[0], result[1])

        _, block_pull = jax.vjp(
            local_block, head_part, b_part, c_part, step_part, decay_rate, start_part
        )
        grads = block_pull((grad_part, carry))
        return (grads[5], grads[:5])

    _, block_grads = lax.scan(
        retreat,
        end_grad,
        (
            head_blocks,
            b_blocks,
            c_blocks,
            step_blocks,
            seg_blocks,
            prev_blocks,
            starts,
            ssd_grad_blocks,
        ),
        reverse=True,
    )
    head_grad = block_grads[0].reshape(count, HEADS, HEAD_DIM) + head_gate_grad
    b_grad = block_grads[1].reshape(count, STATE)
    c_grad = block_grads[2].reshape(count, STATE)
    step_grad = block_grads[3].reshape(count, HEADS)
    rate_grad = jnp.sum(block_grads[4], axis=0)
    ext_grad, raw_grad, conv_w_grad, conv_b_grad, bias_grad, alog_grad = mix_pull(
        (head_grad, b_grad, c_grad, step_grad, rate_grad)
    )
    returned = from_behind(ext_grad[:rim], "grp", -1)
    conv_in_grad = ext_grad[rim:] + jnp.pad(returned, ((count - rim, 0), (0, 0)))
    proj_grad = jnp.concatenate([gate_in_grad, conv_in_grad, raw_grad], axis=1).astype(jnp.bfloat16)
    normed_grad = jnp.dot(proj_grad, full_in.T, preferred_element_type=jnp.float32)
    branch_inputs, igain_grad = pre_pull(normed_grad)
    input_grad = cotangent.astype(jnp.float32) + branch_inputs
    owned = []
    for half in range(2):
        cut = lambda value: lax.slice_in_dim(
            value, half * (value.shape[-1] // 2), (half + 1) * (value.shape[-1] // 2), axis=-1
        ).reshape(-1)
        small = jnp.concatenate(
            [
                cut(igain_grad),
                cut(conv_w_grad),
                cut(conv_b_grad),
                cut(bias_grad),
                cut(alog_grad),
                cut(skip_grad),
                cut(ggain_grad),
            ]
        )
        owned.append(jnp.pad(small, (0, 512 * LANES - small.shape[0])).reshape(512, LANES))
    strip = jnp.concatenate(owned, axis=0).astype(jnp.bfloat16)
    padded = jnp.pad(proj_grad, ((0, 0), (0, W_IN_COLS - proj_grad.shape[1])))
    reduced = reduce_gradients(normed_low, padded, branch_low, cotangent, strip)
    w_in_sum = reduced[:, : proj_grad.shape[1]].astype(jnp.float32)
    w_out_sum = jnp.concatenate(
        [reduced[:, W_IN_COLS : W_IN_COLS + 1024], reduced[:, W_IN_COLS + 1024 :]], axis=0
    ).astype(jnp.float32)
    flat = reduced[:64, W_IN_COLS - LANES : W_IN_COLS].astype(jnp.float32).reshape(-1)
    sizes = (512, 4608, 1152, 16, 16, 16, 1024)
    pieces = []
    start = 0
    for size in sizes:
        pieces.append(flat[start : start + size])
        start += size
    summed = (
        pieces[0],
        w_in_sum,
        pieces[1].reshape(4, 1152),
        pieces[2],
        pieces[3],
        pieces[4],
        pieces[5],
        pieces[6],
        w_out_sum,
    )
    return (
        mixed,
        input_grad,
        summed[0],
        summed[1],
        summed[2],
        summed[3],
        summed[4],
        summed[5],
        summed[6],
        summed[7],
        summed[8],
    )


def solution(mesh):
    placed = (
        P(("rep", "grp"), None),
        P(("rep", "grp")),
        P("grp"),
        P("grp", None),
        P(None, "grp"),
        P("grp"),
        P("grp"),
        P("grp"),
        P("grp"),
        P("grp"),
        P("grp", None),
        P(("rep", "grp"), None),
    )
    return jax.shard_map(
        on_device,
        mesh=mesh,
        in_specs=placed,
        out_specs=(
            P(("rep", "grp"), None),
            P(("rep", "grp"), None),
            P("grp"),
            P("grp", None),
            P(None, "grp"),
            P("grp"),
            P("grp"),
            P("grp"),
            P("grp"),
            P("grp"),
            P("grp", None),
        ),
        check_vma=False,
    )
```

```python
import jax
import jax.numpy as jnp
from jax import lax
from jax.experimental import pallas as pl
from jax.experimental.pallas import tpu as pltpu
from jax.sharding import PartitionSpec as P

EPS = 1e-05
SEQ = 512
OWN = 1024
MIX = 1280
HELD = 2432
EXACT = lax.Precision.HIGHEST
FAR = -1e30


def dot(left, right, over=(1, 0), exact=False):
    return lax.dot_general(
        left,
        right,
        (((over[0],), (over[1],)), ((), ())),
        preferred_element_type=jnp.float32,
        precision=EXACT if exact else None,
    )


def split(value, count):
    parts, rest = [], value
    for _ in range(count):
        parts.append(rest.astype(jnp.bfloat16))
        rest = rest - parts[-1].astype(jnp.float32)
    return parts


def pick(left, chosen, count, over=0):
    parts = jnp.concatenate(split(left, count), axis=1)
    return dot(parts, jnp.concatenate([chosen] * count, axis=over), (1, over))


def summed(chosen, right):
    width = right.shape[1]
    total = dot(chosen, jnp.concatenate(split(right, 3), axis=1))
    return total[:, 0:width] + total[:, width : 2 * width] + total[:, 2 * width :]


def near_exact(left, right, over):
    (a, b), (c, d) = split(left, 2), split(right, 2)
    joined = jnp.concatenate([a, a, b], axis=1)
    return dot(joined, jnp.concatenate([c, d, c], axis=over), (1, over))


def iota(shape, axis):
    return lax.broadcasted_iota(jnp.int32, shape, axis)


def turned(value):
    return jnp.transpose(value)


def layer_kernel(
    grp,
    cot_ready,
    exchange,
    send_mixed,
    send_pg,
    proj,
    vec,
    seg,
    tokens,
    cot,
    w_out,
    w_in,
    branch_out,
    pg_out,
    ng_out,
    strip_out,
    vecs_out,
    turned_branch,
    turned_pg,
    act,
    pre,
    same,
    spread,
    run_t,
    scores,
    bias,
    low_x,
    y,
    bg,
    low_dy,
    turned_dy,
    turned_dx,
    d_scores,
    strip,
    stats,
    far_stats,
):
    f32, bf16 = jnp.float32, jnp.bfloat16
    tile = lambda at: pl.ds(pl.multiple_of(128 * at, 128), 128)
    seg_row = seg[0:1, :].astype(f32)
    seg_col = turned(jnp.broadcast_to(seg_row, (128, SEQ)))
    places = iota((SEQ, 128), 0)
    for k in range(1, 4):
        behind = pltpu.roll(seg_col, k, 0)
        same[k - 1] = jnp.where((places >= k) & (behind == seg_col), 1.0, 0.0)
    rows, cols = iota((SEQ, SEQ), 0), iota((SEQ, SEQ), 1)
    seg_wide = jnp.concatenate([seg_col] * 4, axis=1)
    bias[...] = jnp.where((rows >= cols) & (seg_wide == seg_row), 0.0, FAR)

    @pl.loop(0, 10)
    def _(j):
        value = proj[:, pl.ds(pl.multiple_of(1024 + 128 * j, 128), 128)]
        total = vec[4:5, tile(j)] + vec[3:4, tile(j)] * value
        for k in range(1, 4):
            total = total + vec[3 - k : 4 - k, tile(j)] * (pltpu.roll(value, k, 0) * same[k - 1])
        pre[:, tile(j)] = total
        act[:, tile(j)] = total * jax.nn.sigmoid(total)

    heads = 16 * grp
    raw = proj[:, 2304:2432] + vec[6:7, 0:128]
    step = jnp.maximum(raw, 0.0) + jnp.log1p(jnp.exp(-jnp.abs(raw)))
    rate = -jnp.exp(vec[7:8, 0:128])
    down = jnp.where(rows >= cols, 1.0, 0.0).astype(bf16)
    running = summed(down, step * rate)
    run_t[...] = turned(running)
    widen = jnp.where(iota((128, 2048), 0) == heads + iota((128, 2048), 1) // 128, 1.0, 0.0)
    spread[...] = pick(running, widen.astype(bf16), 3)
    expand = jnp.where(iota((128, OWN), 0) == heads + iota((128, OWN), 1) // 64, 1.0, 0.0)
    expand = expand.astype(bf16)
    step_wide = pick(step, expand, 2)
    skip_wide = pick(jnp.broadcast_to(vec[8:9, 0:128], (8, 128)), expand, 2)[0:1]
    low_x[...] = (act[:, 0:OWN] * step_wide).astype(bf16)
    b_mat, c_mat = act[:, 1024:1152], act[:, 1152:1280]
    scores[...] = near_exact(c_mat, b_mat, 1)
    left_lanes = iota((256, 128), 1) < 64

    def decay(head, i, j):
        mine = spread[256 * i : 256 * i + 256, tile(head)]
        theirs = run_t[pl.ds(heads + head, 1), 256 * j : 256 * j + 256]
        mine = jnp.concatenate([mine, mine], axis=1)
        return jnp.exp(mine - theirs + bias[256 * i : 256 * i + 256, 256 * j : 256 * j + 256])

    def block(i, j):
        return (slice(256 * i, 256 * i + 256), slice(256 * j, 256 * j + 256))

    @pl.loop(0, 8)
    def _(p):
        for i in range(2):
            parts = []
            for e in range(2):
                total = None
                for j in range(i + 1):
                    weight = (decay(2 * p + e, i, j) * scores[block(i, j)]).astype(bf16)
                    term = dot(weight, low_x[256 * j : 256 * j + 256, tile(p)])
                    total = term if total is None else total + term
                parts.append(total)
            y[256 * i : 256 * i + 256, tile(p)] = jnp.where(left_lanes, parts[0], parts[1])

    cot_ready()
    bg[...] = dot(cot[...], w_out[...], (1, 1))
    squares = jnp.zeros((SEQ, 128), f32)
    crosses = jnp.zeros((SEQ, 128), f32)
    for j in range(8):
        at = slice(128 * j, 128 * j + 128)
        gate = proj[:, at]
        full = y[:, at] + skip_wide[:, at] * act[:, at]
        gated = full * (gate * jax.nn.sigmoid(gate))
        squares = squares + gated * gated
        crosses = crosses + bg[:, at] * vec[5:6, at] * gated
    ones = jnp.ones((8, 128), f32)
    first = dot(ones, squares, (1, 1), exact=True)
    second = dot(ones, crosses, (1, 1), exact=True)
    stats[...] = jnp.where(iota((8, SEQ), 0) == 0, first, second)
    exchange()
    whole = (stats[...] + far_stats[...]) * (1.0 / 2048)
    root_row = lax.rsqrt(whole[0:1] + EPS)
    cross_row = whole[1:2] * root_row * root_row
    root = turned(jnp.broadcast_to(root_row, (128, SEQ)))
    cross = turned(jnp.broadcast_to(cross_row, (128, SEQ)))

    strip[...] = jnp.zeros((1024, 128), f32)
    skip_sum = []
    for j in range(8):
        at = slice(128 * j, 128 * j + 128)
        gate = proj[:, at]
        sig = jax.nn.sigmoid(gate)
        opened = gate * sig
        full = y[:, at] + skip_wide[:, at] * act[:, at]
        gated = full * opened
        scaled = gated * root
        branch_out[:, at] = (scaled * vec[5:6, at]).astype(bf16)
        back = bg[:, at]
        strip[pl.ds(512 * grp + 49 + j, 1), :] = jnp.sum(back * scaled, axis=0, keepdims=True)
        d_gated = root * (back * vec[5:6, at] - gated * cross)
        d_full = d_gated * opened
        d_gate = d_gated * full * (sig * (1.0 + gate * (1.0 - sig)))
        pg_out[:, at] = d_gate.astype(bf16)
        bg[:, at] = d_full
        low_dy[:, at] = d_full.astype(bf16)
        skip_sum.append(jnp.sum(d_full * act[:, at], axis=0, keepdims=True))
    turned_dy[...] = turned(low_dy[...])
    turned_branch[...] = turned(branch_out[...])
    send_mixed()

    d_scores[...] = jnp.zeros((SEQ, SEQ), f32)

    @pl.loop(0, 8)
    def _(p):
        for e in range(2):
            head = 2 * p + e
            own = pl.ds(pl.multiple_of(64 * head, 64), 64)
            sums = [None, None]
            for i in range(2):
                at_i = slice(256 * i, 256 * i + 256)
                out_grad = low_dy[at_i, tile(p)]
                keep = left_lanes if e == 0 else ~left_lanes
                out_grad = jnp.where(keep, out_grad, jnp.zeros_like(out_grad))
                for j in range(i + 1):
                    near = decay(head, i, j)
                    weight = (near * scores[block(i, j)]).astype(bf16)
                    d_weight = dot(out_grad, low_x[256 * j : 256 * j + 256, tile(p)], (1, 1))
                    d_scores[block(i, j)] += d_weight * near
                    term = dot(turned_dy[own, at_i], weight)
                    sums[j] = term if sums[j] is None else sums[j] + term
            for j in range(2):
                turned_dx[own, 256 * j : 256 * j + 256] = sums[j]

    d_x = turned(turned_dx[...])
    dots = low_dy[...].astype(f32) * y[...] - low_x[...].astype(f32) * d_x
    d_run = pick(dots, expand, 3, 1)
    up = jnp.where(rows <= cols, 1.0, 0.0).astype(bf16)
    d_log = summed(up, d_run)
    d_step = pick(d_x * act[:, 0:OWN], expand, 2, 1) + d_log * rate
    d_raw = d_step * jax.nn.sigmoid(raw)
    pg_out[:, 2304:2432] = d_raw.astype(bf16)
    skip_row = pick(jnp.broadcast_to(jnp.concatenate(skip_sum, axis=1), (8, OWN)), expand, 3, 1)[0:1]
    for half in range(2):
        base = 512 * half
        strip[base + 57 : base + 58, :] = jnp.sum(d_raw, axis=0, keepdims=True)
        strip[base + 58 : base + 59, :] = jnp.sum(d_log * step, axis=0, keepdims=True) * rate
        strip[base + 59 : base + 60, :] = skip_row
    d_b = near_exact(turned(d_scores[...]), c_mat, 0)
    d_c = near_exact(d_scores[...], b_mat, 0)
    act[:, 0:OWN] = d_x * step_wide + bg[...] * skip_wide
    act[:, 1024:1152] = d_b
    act[:, 1152:1280] = d_c

    @pl.loop(0, 10)
    def _(j):
        value = proj[:, pl.ds(pl.multiple_of(1024 + 128 * j, 128), 128)]
        before = pre[:, tile(j)]
        sig = jax.nn.sigmoid(before)
        d_pre = act[:, tile(j)] * (sig * (1.0 + before * (1.0 - sig)))
        total = vec[3:4, tile(j)] * d_pre
        full_tile = jnp.where(j < 8, 8 * grp + j, 8 + j)
        half = full_tile // 9
        base = 512 * half + full_tile - 9 * half
        strip[pl.ds(base + 31, 1), :] = jnp.sum(d_pre * value, axis=0, keepdims=True)
        strip[pl.ds(base + 40, 1), :] = jnp.sum(d_pre, axis=0, keepdims=True)
        for k in range(1, 4):
            kept = pltpu.roll(d_pre * same[k - 1], SEQ - k, 0)
            total = total + vec[3 - k : 4 - k, tile(j)] * kept
            strip[pl.ds(base + 4 + 9 * (3 - k), 1), :] = jnp.sum(
                kept * value, axis=0, keepdims=True
            )
        pg_out[:, pl.ds(pl.multiple_of(1024 + 128 * j, 128), 128)] = total.astype(bf16)

    pg_out[:, HELD:] = jnp.zeros((SEQ, 128), bf16)
    turned_pg[...] = turned(pg_out[...])
    send_pg()
    normed_grad = dot(pg_out[...], w_in[...])
    ng_out[...] = normed_grad.astype(ng_out.dtype)
    inputs = tokens[...].astype(f32)
    scale = lax.rsqrt(jnp.mean(inputs * inputs, axis=1, keepdims=True) + EPS)
    gain_row = jnp.sum(normed_grad * (inputs * scale), axis=0, keepdims=True)
    for j in range(8):
        strip[512 * (j // 4) + j % 4 : 512 * (j // 4) + j % 4 + 1, :] = gain_row[
            :, 128 * j : 128 * j + 128
        ]
    strip_out[...] = turned(strip[...]).astype(bf16)
    vecs_out[0] = strip[0:64, :]
    vecs_out[1] = strip[512:576, :]


def layer_body(
    tokens, seg, small, w_in, w_out, cot_own,
    turned_branch, mixed_out, turned_pg, ng_out, strip_out, normed_out, cot_out, vecs_out,
    far_branch, far_pg, far_normed, far_cot,
    branch_out, pg_out, proj, vec, words, sent_mixed, far_mixed, *scratch,
):
    f32, bf16 = jnp.float32, jnp.bfloat16
    send_sems, recv_sems = scratch[-2:]
    scratch = scratch[:-2]
    stats, far_stats = scratch[-2:]
    here = place()
    grp = here["grp"]
    across = device_at(moved(here, "z", 2))
    twin = twin_of(here)
    theirs = 1 - here["core"]
    greet([across, twin])
    copies = Copies(send_sems, recv_sems)
    own_rows = pl.ds(pl.multiple_of(256 * grp, 256), 256)
    far_rows = pl.ds(pl.multiple_of(256 * (1 - grp), 256), 256)
    cot_in = copies.start(cot_own, cot_out.at[own_rows, :], across)
    cot_out[own_rows, :] = cot_own[...]

    words[...] = small[...].astype(f32)
    for j in range(10):
        if j < 8:
            half = lax.div(8 * grp + j, 9)
            at = 8 * grp + j - 9 * half
        else:
            half, at = 1, j - 1
        for k in range(5):
            vec[k : k + 1, 128 * j : 128 * j + 128] = words[half, pl.ds(4 + 9 * k + at, 1), :]
        if j < 8:
            vec[5:6, 128 * j : 128 * j + 128] = words[grp, 49 + j : 50 + j, :]
            vec[9:10, 128 * j : 128 * j + 128] = words[j // 4, j % 4 : j % 4 + 1, :]
    for k in range(3):
        vec[6 + k : 7 + k, 0:128] = words[0, 57 + k : 58 + k, :] + words[1, 57 + k : 58 + k, :]
    inputs = tokens[...].astype(f32)
    scale = lax.rsqrt(jnp.mean(inputs * inputs, axis=1, keepdims=True) + EPS)
    normed_out[...] = (inputs * scale * vec[9:10, 0:1024]).astype(bf16)

    held = {"normed": copies.start(normed_out, far_normed, twin)}

    @pl.loop(0, 9)
    def _(j):
        at = pl.ds(pl.multiple_of(256 * j, 256), 256)
        proj[:, at] = dot(normed_out[...], w_in[at, :], (1, 1))

    proj[:, 2304:2432] = dot(normed_out[...], w_in[2304:2432, :], (1, 1))

    def cot_ready():
        cot_in.wait_recv()
        half = pl.ds(pl.multiple_of(512 * theirs, 512), 512)
        held["cot"] = copies.start(cot_out.at[:, half], far_cot, twin)

    def exchange():
        copy = copies.start(stats, far_stats, across)
        copy.wait_recv()

    def send_pg():
        rows = pl.ds(pl.multiple_of(1280 * theirs, 1280), 1280)
        held["pg"] = copies.start(turned_pg.at[rows, :], far_pg, twin)

    def send_mixed():
        held["branch"] = copies.start(turned_branch, far_branch, twin)
        sent_mixed[...] = dot(branch_out[far_rows, :], w_out[...]).astype(bf16)
        held["mixed"] = copies.start(sent_mixed, far_mixed, across)

    layer_kernel(
        grp, cot_ready, exchange, send_mixed, send_pg, proj, vec, seg, tokens, cot_out, w_out, w_in,
        branch_out, pg_out, ng_out, strip_out, vecs_out, turned_branch, turned_pg, *scratch,
    )
    held["mixed"].wait_recv()
    total = dot(branch_out[own_rows, :], w_out[...]) + far_mixed[...].astype(f32)
    total = total + tokens[own_rows, :].astype(f32)
    mixed_out[...] = total.astype(bf16)
    for name in ("normed", "cot", "branch", "pg"):
        held[name].wait_recv()
    copies.finish()


def layer_grads(tokens, seg, small, w_in, w_out, cotangent):
    f32, bf16 = jnp.float32, jnp.bfloat16
    shape = jax.ShapeDtypeStruct
    spec = pl.BlockSpec(memory_space=pltpu.VMEM)
    scratch = [
        pltpu.VMEM((SEQ, OWN), bf16),
        pltpu.VMEM((SEQ, 2560), bf16),
        pltpu.VMEM((SEQ, HELD), f32),
        pltpu.VMEM((16, MIX), f32),
        pltpu.VMEM((2, 64, 128), f32),
        pltpu.VMEM((256, 1024), bf16),
        pltpu.VMEM((256, 1024), bf16),
    ]
    return pl.pallas_call(
        layer_body,
        out_shape=[
            shape((OWN, SEQ), bf16),
            shape((256, 1024), bf16),
            shape((2560, SEQ), bf16),
            shape((SEQ, 1024), bf16),
            shape((128, 1024), bf16),
            shape((SEQ, 1024), bf16),
            shape((SEQ, 1024), bf16),
            shape((2, 64, 128), f32),
            shape((OWN, SEQ), bf16),
            shape((1280, SEQ), bf16),
            shape((SEQ, 1024), bf16),
            shape((SEQ, 512), bf16),
        ],
        in_specs=[spec] * 6,
        out_specs=[spec] * 8 + [pl.BlockSpec(memory_space=pl.ANY)] * 4,
        scratch_shapes=scratch + layer_scratch() + copy_sems(8),
        compiler_params=pltpu.CompilerParams(
            collective_id=1, has_side_effects=True, vmem_limit_bytes=62 * 1024 * 1024
        ),
        name="layer_grads",
    )(tokens, seg, small, w_in, w_out, cotangent)


def layer_scratch():
    f32, bf16 = jnp.float32, jnp.bfloat16
    return [
        pltpu.VMEM((SEQ, MIX), f32),
        pltpu.VMEM((SEQ, MIX), f32),
        pltpu.VMEM((3, SEQ, 128), f32),
        pltpu.VMEM((SEQ, 2048), f32),
        pltpu.VMEM((128, SEQ), f32),
        pltpu.VMEM((SEQ, SEQ), f32),
        pltpu.VMEM((SEQ, SEQ), f32),
        pltpu.VMEM((SEQ, OWN), bf16),
        pltpu.VMEM((SEQ, OWN), f32),
        pltpu.VMEM((SEQ, OWN), f32),
        pltpu.VMEM((SEQ, OWN), bf16),
        pltpu.VMEM((OWN, SEQ), bf16),
        pltpu.VMEM((OWN, SEQ), f32),
        pltpu.VMEM((SEQ, SEQ), f32),
        pltpu.VMEM((1024, 128), f32),
        pltpu.VMEM((8, SEQ), f32),
        pltpu.VMEM((8, SEQ), f32),
    ]


MESH = pl.DeviceIdType.MESH


def place():
    rep, grp = lax.axis_index("rep"), lax.axis_index("grp")
    return {
        "core": lax.rem(rep, 2),
        "x": lax.rem(lax.div(rep, 2), 4),
        "y": lax.rem(lax.div(rep, 8), 4),
        "z": 2 * grp + lax.div(rep, 32),
        "low": lax.div(rep, 32),
        "grp": grp,
    }


def device_at(here):
    low_z = lax.rem(here["z"], 2)
    rep = ((low_z * 4 + here["y"]) * 4 + here["x"]) * 2 + here["core"]
    return (rep, lax.div(here["z"], 2))


def moved(here, axis, by):
    return dict(here, **{axis: lax.rem(here[axis] + (by % 4), 4)})


def twin_of(here):
    return device_at(dict(here, core=1 - here["core"]))


def mate_of(here):
    return device_at(dict(here, z=here["z"] + 1 - 2 * here["low"]))


def greet(partners):
    barrier = pltpu.get_barrier_semaphore()
    for partner in partners:
        pl.semaphore_signal(barrier, inc=1, device_id=partner, device_id_type=MESH)
    pl.semaphore_wait(barrier, len(partners))


class Copies:
    def __init__(self, send_sems, recv_sems):
        self.send_sems, self.recv_sems = send_sems, recv_sems
        self.made = []

    def start(self, src, dst, device):
        at = len(self.made)
        copy = pltpu.make_async_remote_copy(
            src_ref=src,
            dst_ref=dst,
            send_sem=self.send_sems.at[at],
            recv_sem=self.recv_sems.at[at],
            device_id=device,
            device_id_type=MESH,
        )
        copy.start()
        self.made.append(copy)
        return copy

    def finish(self):
        for copy in self.made:
            copy.wait_send()


def copy_sems(count):
    return [pltpu.SemaphoreType.DMA((count,)), pltpu.SemaphoreType.DMA((count,))]


def cut_in_two(axes, free, sizes):
    if not free:
        return (axes, None)
    name = free[0]
    half = sizes[name] // 2
    return (
        dict(axes, **{name: slice(0, half)}),
        dict(axes, **{name: slice(half, 2 * half)}),
    )


class Spread:
    def __init__(self, copies, here, order, view, sizes, others):
        self.copies, self.here, self.order, self.view, self.sizes = copies, here, order, view, sizes
        self.own = {"x": here["x"], "y": here["y"], "z": here["low"]}
        self.own = {name: self.own[name] for name in order + others}
        self.twin = twin_of(here)
        self.to_twin = []

    def axes(self, stage, at):
        axes = dict(self.own)
        for name in self.order[:stage]:
            axes[name] = slice(None)
        axes[self.order[stage]] = at
        return axes

    def free(self, stage):
        return [name for name in ("x", "y", "z") if name in self.order[:stage]]

    def share(self, stage, at):
        if stage == len(self.order) - 1:
            piece = self.view(self.axes(stage, at))
            self.to_twin.append(self.copies.start(piece, piece, self.twin))

    def begin(self, stage):
        axis = self.order[stage]
        at = self.own[axis]
        piece = self.view(self.axes(stage, at))
        if axis == "z":
            self.first = (self.copies.start(piece, piece, mate_of(self.here)),)
        else:
            self.first = (
                self.copies.start(piece, piece, device_at(moved(self.here, axis, 1))),
                self.copies.start(piece, piece, device_at(moved(self.here, axis, -1))),
            )
        self.share(stage, at)

    def forward(self, stage):
        axis = self.order[stage]
        self.second = []
        if axis == "z":
            self.first[0].wait_recv()
            self.share(stage, 1 - self.own[axis])
            return
        free = self.free(stage)
        before, after = lax.rem(self.own[axis] + 3, 4), lax.rem(self.own[axis] + 1, 4)
        self.first[0].wait_recv()
        low, _ = cut_in_two(self.axes(stage, before), free, self.sizes)
        piece = self.view(low)
        self.second.append(self.copies.start(piece, piece, device_at(moved(self.here, axis, 1))))
        self.share(stage, before)
        self.first[1].wait_recv()
        if free:
            _, high = cut_in_two(self.axes(stage, after), free, self.sizes)
            piece = self.view(high)
            self.second.append(
                self.copies.start(piece, piece, device_at(moved(self.here, axis, -1)))
            )
        self.share(stage, after)

    def complete(self, stage):
        for copy in self.second:
            copy.wait_recv()
        if self.order[stage] != "z":
            self.share(stage, lax.rem(self.own[self.order[stage]] + 2, 4))


def gather_kernel(
    w_ref, small_ref, seg_ref, tok_ref, w_out, small_out, seg_out, tok_out,
    staged, relayed, local_sems, send_sems, recv_sems,
):
    here = place()
    grp, core = here["grp"], here["core"]
    away = 1 - grp
    across = device_at(moved(here, "z", 2))
    beside = device_at(dict(here, z=3 - here["z"]))
    ring = [device_at(moved(here, axis, by)) for axis in ("x", "y") for by in (1, -1)]
    lanes = lambda half, first, width: pl.ds(pl.multiple_of(512 * half + first, 128), width)

    kept = []

    def keep(owner, dst):
        for start, rows, at in ((1024 * owner, 1024, 0), (2048 + 1024 * owner, 1024, 1024), (4096, 288, 2048)):
            src = w_ref.at[pl.ds(pl.multiple_of(start, 32), rows), :]
            copy = pltpu.make_async_copy(src, dst(pl.ds(at, rows)), local_sems.at[len(kept)])
            copy.start()
            kept.append(copy)

    keep(away, lambda rows: staged.at[rows, :])
    keep(grp, lambda rows: w_out.at[rows, lanes(grp, 0, 512)])
    staged[2336:2560, :] = jnp.zeros((224, 512), jnp.bfloat16)
    w_out[2336:2560, lanes(grp, 0, 512)] = jnp.zeros((224, 512), jnp.bfloat16)
    by_core = 1 + 2 * core
    onward = device_at(dict(here, z=lax.rem(here["z"] + by_core, 4)))
    sides = [device_at(moved(here, "z", by)) for by in (1, -1)]
    greet([across, twin_of(here)] + sides + ring)
    copies = Copies(send_sems, recv_sems)
    tok_rows = pl.ds(pl.multiple_of(256 * grp, 256), 256)
    for copy in kept[0:3]:
        copy.wait()
    orders = (("y", "x"), ("x", "y"))

    def rows_of(part, axes):
        minor, major = orders[part]
        start, count = axes[minor], 1
        if isinstance(start, slice):
            bounds = start.indices(4)
            start, count = bounds[0], bounds[1] - bounds[0]
        return pl.ds(
            pl.multiple_of(1280 * core + 320 * axes[major] + 80 * start, 16), 80 * count
        )

    pieces = []
    for part in range(2):
        rows = rows_of(part, here)
        pieces.append(
            copies.start(
                staged.at[rows, pl.ds(256 * part, 256)],
                w_out.at[rows, lanes(grp, 256 * part, 256)],
                beside,
            )
        )
    quarter = lambda at: pl.ds(64 * at, 64)
    tok_hops = [
        copies.start(tok_ref.at[quarter(at), :], relayed.at[quarter(at), :], onward)
        for at in range(4)
    ]
    tok_in = []

    def relay(at):
        tok_hops[at].wait_recv()
        owner = lax.div(lax.rem(here["z"] + 4 - by_core, 4), 2)
        rows = pl.ds(pl.multiple_of(256 * owner + 64 * at, 64), 64)
        tok_in.append(copies.start(relayed.at[quarter(at), :], tok_out.at[rows, :], onward))

    small_in = copies.start(small_ref, small_out.at[grp], beside)
    seg_in = copies.start(seg_ref, seg_out.at[:, tok_rows], across)
    tok_out[tok_rows, :] = tok_ref[...]
    small_out[grp] = small_ref[...]
    seg_out[:, tok_rows] = seg_ref[...]
    sizes = {"x": 4, "y": 4}
    parts = []
    for part in range(2):

        def view(axes, part=part):
            return w_out.at[rows_of(part, axes), lanes(away, 256 * part, 256)]

        parts.append(Spread(copies, here, orders[part], view, sizes, ()))
    for piece in pieces:
        piece.wait_recv()
    for stage in range(2):
        for part in parts:
            part.begin(stage)
        relay(2 * stage)
        for part in parts:
            part.forward(stage)
        relay(2 * stage + 1)
        for part in parts:
            part.complete(stage)
    for part in parts:
        for copy in part.to_twin:
            copy.wait_recv()
    for copy in tok_in + [small_in, seg_in]:
        copy.wait_recv()
    for copy in kept[3:]:
        copy.wait()
    copies.finish()


def gather(w_in, small, seg, tokens):
    bf16 = jnp.bfloat16
    vmem = pl.BlockSpec(memory_space=pltpu.VMEM)
    return pl.pallas_call(
        gather_kernel,
        out_shape=[
            jax.ShapeDtypeStruct((2560, 1024), bf16),
            jax.ShapeDtypeStruct((2, 64, 128), bf16),
            jax.ShapeDtypeStruct((8, SEQ), jnp.int32),
            jax.ShapeDtypeStruct((SEQ, 1024), bf16),
        ],
        in_specs=[pl.BlockSpec(memory_space=pl.ANY)] + [vmem] * 3,
        out_specs=[vmem] * 4,
        scratch_shapes=[pltpu.VMEM((2560, 512), bf16), pltpu.VMEM((256, 1024), bf16), pltpu.SemaphoreType.DMA((6,))] + copy_sems(40),
        compiler_params=pltpu.CompilerParams(
            collective_id=0, has_side_effects=True, vmem_limit_bytes=60 * 1024 * 1024
        ),
        name="gather",
    )(w_in.T, small, seg, tokens)


W_PARTS = (("x", "y"), ("y", "x"))


def reduce_kernel(
    normed_ref, pg_ref, branch_ref, cot_ref, strip_ref, ng_ref,
    far_branch_ref, far_pg_ref, far_normed_ref, far_cot_ref, out_w, out_o, far_ng,
    near_normed, near_pg, near_branch, near_cot, near_strip,
    far_normed, far_pg, far_branch, far_cot, far_strip, buf_w, buf_o,
    half_0, whole_0, half_1, whole_1, last, half_o, whole_o, pair_o, last_o,
    local_sems, send_sems, recv_sems,
):
    f32, bf16 = jnp.float32, jnp.bfloat16
    here = place()
    grp, core, low = here["grp"], here["core"], here["low"]
    twin, mate = twin_of(here), mate_of(here)
    crossing = [device_at(moved(here, "z", by)) for by in (1, 2, 3)]
    ring = [device_at(moved(here, axis, by)) for axis in ("x", "y") for by in (1, -1)]
    greet([twin] + crossing + ring)
    copies = Copies(send_sems, recv_sems)

    loads = []
    for at, (src, dst) in enumerate(
        (
            (branch_ref, near_branch),
            (cot_ref.at[:, pl.ds(pl.multiple_of(512 * core, 512), 512)], near_cot),
            (far_branch_ref, far_branch),
            (far_cot_ref, far_cot),
            (normed_ref, near_normed),
            (far_normed_ref, far_normed),
            (far_pg_ref, far_pg),
            (pg_ref.at[pl.ds(pl.multiple_of(1280 * core, 1280), 1280), :], near_pg),
            (strip_ref, near_strip),
        )
    ):
        loads.append(pltpu.make_async_copy(src, dst, local_sems.at[at]))
        loads[-1].start()
    my_half = pl.ds(pl.multiple_of(512 * core, 512), 512)
    strip_in = copies.start(strip_ref, far_strip, twin)

    sizes = {"x": 4, "y": 4, "z": 4}

    def ring_axes(axis, axes, by):
        return dict(axes, **{axis: lax.rem(here[axis] + (by % 4), 4)})

    class RingSum:
        def __init__(self, axis, axes, free, view, load, store, halved, whole):
            self.axis, self.axes, self.free = axis, axes, free
            self.view, self.load, self.store = view, load, store
            self.halved, self.whole = halved, whole
            self.ahead = device_at(moved(here, axis, 1))
            self.behind = device_at(moved(here, axis, -1))

        def chunk(self, by):
            return ring_axes(self.axis, self.axes, by)

        def begin(self):
            first, second = cut_in_two(self.chunk(2), self.free, sizes)
            if self.free:
                self.a = copies.start(self.view(first), self.halved.at[0], self.ahead)
                self.b = copies.start(self.view(second), self.halved.at[1], self.behind)
                _, second = cut_in_two(self.chunk(1), self.free, sizes)
                first, _ = cut_in_two(self.chunk(-1), self.free, sizes)
                self.waits = [
                    copies.start(self.view(second), self.whole.at[0, pl.ds(2, 2)], self.ahead),
                    copies.start(self.view(first), self.whole.at[1, pl.ds(0, 2)], self.behind),
                ]
            else:
                self.a = copies.start(self.view(first), self.whole.at[2], self.ahead)
                self.waits = [copies.start(self.view(self.chunk(-1)), self.whole.at[1], self.behind)]

        def add(self, axes, incoming):
            total = self.load(axes).astype(f32)
            for value in incoming:
                total = total + value.astype(f32)
            self.store(axes, total.astype(bf16))

        def relay(self):
            self.a.wait_recv()
            if self.free:
                first, _ = cut_in_two(self.chunk(1), self.free, sizes)
                self.add(first, [self.halved[0]])
                self.waits.append(
                    copies.start(self.view(first), self.whole.at[0, pl.ds(0, 2)], self.ahead)
                )
                self.b.wait_recv()
                _, second = cut_in_two(self.chunk(-1), self.free, sizes)
                self.add(second, [self.halved[1]])
                self.waits.append(
                    copies.start(self.view(second), self.whole.at[1, pl.ds(2, 2)], self.behind)
                )
            else:
                self.add(self.chunk(1), [self.whole[2]])
                self.waits.append(
                    copies.start(self.view(self.chunk(1)), self.whole.at[0], self.ahead)
                )

        def settle(self):
            for copy in self.waits:
                copy.wait_recv()
            self.add(self.chunk(0), [self.whole[0], self.whole[1]])

    def w_ring(part, stage):
        order = W_PARTS[part]
        axes = {"z": slice(None)}
        if stage == 0:
            axes[order[1]] = slice(None)
        else:
            axes[order[0]] = here[order[0]]
        free = [name for name in ("x", "y", "z") if name in axes and isinstance(axes[name], slice)]
        index = lambda axes: (part, axes["x"], axes["y"], axes["z"])

        def load(axes):
            return buf_w[index(axes)]

        def store(axes, value):
            buf_w[index(axes)] = value

        half, whole = ((half_0, whole_0), (half_1, whole_1))[stage]
        return RingSum(
            order[stage], axes, free, lambda axes: buf_w.at[index(axes)], load, store,
            half.at[part], whole.at[part],
        )

    def o_ring(stage):
        axis = ("x", "y")[stage]
        axes = {"y": slice(None)} if stage == 0 else {"x": here["x"]}
        free = ["y"] if stage == 0 else []
        index = lambda axes: (axes["x"], axes["y"], low)

        def load(axes):
            return buf_o[index(axes)]

        def store(axes, value):
            buf_o[index(axes)] = value

        return RingSum(
            axis, axes, free, lambda axes: buf_o.at[index(axes)], load, store,
            half_o, (whole_o, last_o)[stage],
        )

    for copy in loads[0:4]:
        copy.wait()

    @pl.loop(0, 4)
    def _(row):
        at = pl.ds(pl.multiple_of(256 * row, 256), 256)
        value = dot(near_branch[at, :], near_cot[...])
        value = value + dot(far_branch[at, :], far_cot[...])
        buf_o[row] = value.astype(bf16).reshape(4, 2, 32, 512)

    pair_in = copies.start(buf_o.at[:, :, 1 - low], pair_o, mate)

    for copy in loads[4:]:
        copy.wait()
    strip_in.wait_recv()

    def w_rows(row):
        rows = pl.ds(pl.multiple_of(320 * row, 16), 320)
        return dot(near_pg[rows, :], near_normed[...]) + dot(far_pg[rows, :], far_normed[...])

    def w_store(row, value):
        for part in range(2):
            for z in range(4):
                tile = value[:, 256 * z + 128 * part : 256 * z + 128 * part + 128]
                buf_w[part, row, :, z] = tile.astype(bf16).reshape(4, 80, 128)

    @pl.loop(0, 3)
    def _(row):
        w_store(row, w_rows(row))

    value = w_rows(3)
    small = near_strip[...].astype(f32) + far_strip[...].astype(f32)
    tail = value[192:, :] + small * core.astype(f32)
    w_store(3, jnp.concatenate([value[:192, :], tail], axis=0))
    rings = []
    for part in range(2):
        rings.append(w_ring(part, 0))
        rings[-1].begin()

    pair_in.wait_recv()

    @pl.loop(0, 4)
    def _(row):
        total = buf_o[row, :, low].astype(f32) + pair_o[row].astype(f32)
        buf_o[row, :, low] = total.astype(bf16)

    their_tokens = pl.ds(pl.multiple_of(256 * (1 - grp), 256), 256)
    ng_in = copies.start(ng_ref.at[their_tokens, :], far_ng, crossing[1])
    o_part = o_ring(0)
    o_part.begin()
    for ring_sum in rings:
        ring_sum.relay()
    o_part.relay()
    later = []
    for part in range(2):
        rings[part].settle()
        later.append(w_ring(part, 1))
        later[-1].begin()
    o_part.settle()
    o_part = o_ring(1)
    o_part.begin()
    for ring_sum in later:
        ring_sum.relay()
    o_part.relay()

    across = []
    for part in range(2):
        later[part].settle()
        across.append(
            [
                copies.start(
                    buf_w.at[part, here["x"], here["y"], lax.rem(here["z"] + by, 4)],
                    last.at[part, by - 1],
                    crossing[by - 1],
                )
                for by in (1, 2, 3)
            ]
        )
    o_part.settle()
    out_o[here["x"], here["y"], low, :, my_half] = buf_o[here["x"], here["y"], low]
    o_view = lambda axes: out_o.at[axes["x"], axes["y"], axes["z"], :, my_half]
    out_sizes = {"x": 4, "y": 4, "z": 2}
    o_spread = Spread(copies, here, ("y", "x", "z"), o_view, out_sizes, ())
    o_spread.begin(0)
    spreads = []
    for part in range(2):
        for copy in across[part]:
            copy.wait_recv()
        mine = buf_w[part, here["x"], here["y"], here["z"]].astype(f32)
        mine = mine + last[part, 2 - 2 * low].astype(f32)
        other = last[part, 1].astype(f32) + last[part, 2 * low].astype(f32)
        out_w[grp, core, here["x"], here["y"], low, part] = mine.astype(bf16)
        out_w[1 - grp, core, here["x"], here["y"], low, part] = other.astype(bf16)

        def w_view(axes, part=part):
            return out_w.at[:, core, axes["x"], axes["y"], axes["z"], part]

        order = ("z",) + W_PARTS[part][::-1]
        spreads.append(Spread(copies, here, order, w_view, out_sizes, ()))
        spreads[-1].begin(0)
    spreads.append(o_spread)
    for stage in range(3):
        if stage > 0:
            for spread in spreads:
                spread.begin(stage)
        for spread in spreads:
            spread.forward(stage)
        for spread in spreads:
            spread.complete(stage)
    for spread in spreads:
        for copy in spread.to_twin:
            copy.wait_recv()
    ng_in.wait_recv()
    copies.finish()


def reduce_gradients(normed, proj_grad, branch, cotangent, strip, ng, far):
    bf16 = jnp.bfloat16
    vmem = lambda *shape: pltpu.VMEM(shape, bf16)
    spec = pl.BlockSpec(memory_space=pltpu.VMEM)
    scratch = 2 * [
        vmem(SEQ, 1024),
        vmem(1280, SEQ),
        vmem(OWN, SEQ),
        vmem(SEQ, 512),
        vmem(128, 1024),
    ]
    scratch += [
        vmem(2, 4, 4, 4, 80, 128),
        vmem(4, 4, 2, 32, 512),
        vmem(2, 2, 2, 4, 80, 128),
        vmem(2, 2, 4, 4, 80, 128),
        vmem(2, 2, 2, 80, 128),
        vmem(2, 2, 4, 80, 128),
        vmem(2, 3, 80, 128),
        vmem(2, 2, 32, 512),
        vmem(2, 4, 32, 512),
        vmem(4, 4, 32, 512),
        vmem(3, 32, 512),
    ]
    return pl.pallas_call(
        reduce_kernel,
        out_shape=[
            jax.ShapeDtypeStruct((2, 2, 4, 4, 2, 2, 80, 128), bf16),
            jax.ShapeDtypeStruct((4, 4, 2, 32, 1024), bf16),
            jax.ShapeDtypeStruct((256, 1024), bf16),
        ],
        in_specs=[pl.BlockSpec(memory_space=pl.ANY)] * 10,
        out_specs=[spec] * 3,
        scratch_shapes=scratch + [pltpu.SemaphoreType.DMA((9,))] + copy_sems(110),
        compiler_params=pltpu.CompilerParams(
            collective_id=2, has_side_effects=True, vmem_limit_bytes=60 * 1024 * 1024
        ),
        name="reduce_gradients",
    )(normed, proj_grad, branch, cotangent, strip, ng, *far)

def finish_kernel(
    sum_w, sum_o, ng, far_ng, tokens, cot, small, mixed, vecs_ref,
    w_in_out, w_out_out, input_out, mixed_out, gain_out, conv_w_out, conv_b_out, heads_out, gate_out,
    loaded_w, loaded_o, gate_rows, x_rows, end_rows, o_rows, sems,
):
    f32 = jnp.float32
    grp = lax.axis_index("grp")
    loads = [
        pltpu.make_async_copy(sum_o, loaded_o, sems.at[4]),
        pltpu.make_async_copy(sum_w, loaded_w, sems.at[5]),
    ]
    for copy in loads:
        copy.start()
    started = []

    def send(src, dst):
        copy = pltpu.make_async_copy(src, dst, sems.at[len(started)])
        copy.start()
        started.append(copy)

    def block(own, at):
        core, x, y = at // 16, at // 4 % 4, at % 4
        return lambda q: loaded_w[own, core, x, y, q // 2, q % 2]

    def fill(ref, own, base, first, last):
        for at in range(first // 80, -(-last // 80)):
            low, high = max(first, 80 * at), min(last, 80 * at + 80)
            for q in range(4):
                part = block(own, at)(q)[low - 80 * at : high - 80 * at].astype(f32)
                ref[base + low - first : base + high - first, 128 * q : 128 * q + 128] = part

    own_rows = pl.ds(pl.multiple_of(256 * grp, 256), 256)
    words = small[...].astype(f32)
    gain = jnp.concatenate([words[j // 4, j % 4 : j % 4 + 1] for j in range(8)], axis=1)
    inputs = tokens[...].astype(f32)
    scale = lax.rsqrt(jnp.mean(inputs * inputs, axis=1, keepdims=True) + EPS)
    scaled = (ng[own_rows, :].astype(f32) + far_ng[...].astype(f32)) * gain
    inner = jnp.mean(scaled * inputs, axis=1, keepdims=True)
    input_out[...] = cot[...].astype(f32) + scale * (scaled - inputs * (scale * scale * inner))
    mixed_out[...] = mixed[...]
    loads[0].wait()
    for row in range(4):
        o_rows[256 * row : 256 * row + 256, :] = loaded_o[row].reshape(256, 1024).astype(f32)
    send(o_rows, w_out_out)
    loads[1].wait()
    for own in range(2):
        fill(gate_rows, own, 1024 * own, 0, 1024)
    send(gate_rows, w_in_out.at[pl.ds(0, 2048), :])
    for own in range(2):
        fill(x_rows, own, 1024 * own, 1024, 2048)
    send(x_rows, w_in_out.at[pl.ds(2048, 2048), :])
    fill(end_rows, 0, 0, 2048, 2560)
    for at in range(25, 32):
        low = max(2048, 80 * at)
        for q in range(4):
            part = block(1, at)(q)[low - 80 * at :].astype(f32)
            end_rows[low - 2048 : 80 * at + 80 - 2048, 128 * q : 128 * q + 128] += part
    send(end_rows.at[pl.ds(0, 288), :], w_in_out.at[pl.ds(4096, 288), :])
    vecs = vecs_ref[...]
    for j in range(4):
        gain_out[j : j + 1, :] = vecs[j : j + 1]
        for k in range(9):
            conv_w_out[j : j + 1, 128 * k : 128 * k + 128] = vecs[4 + 9 * j + k : 5 + 9 * j + k]
    for k in range(9):
        conv_b_out[0:1, 128 * k : 128 * k + 128] = vecs[40 + k : 41 + k]
    gate_out[...] = vecs[49:57]
    heads = vecs[56:64]
    heads_out[...] = jnp.where(grp == 0, heads, pltpu.roll(heads, 112, 1))

    for copy in started:
        copy.wait()


def finish(sum_w, sum_o, ng, far_ng, tokens, cot, small, mixed, vecs):
    f32 = jnp.float32
    shape = jax.ShapeDtypeStruct
    spec = pl.BlockSpec(memory_space=pltpu.VMEM)
    away = pl.BlockSpec(memory_space=pl.ANY)
    return pl.pallas_call(
        finish_kernel,
        out_shape=[
            shape((4384, 512), f32),
            shape((1024, 1024), f32),
            shape((256, 1024), f32),
            shape((256, 1024), jnp.bfloat16),
            shape((4, 128), f32),
            shape((4, 1152), f32),
            shape((1, 1152), f32),
            shape((8, 128), f32),
            shape((8, 128), f32),
        ],
        in_specs=[away] * 2 + [spec] * 7,
        out_specs=[away] * 2 + [spec] * 7,
        scratch_shapes=[
            pltpu.VMEM((2, 2, 4, 4, 2, 2, 80, 128), jnp.bfloat16),
            pltpu.VMEM((4, 4, 2, 32, 1024), jnp.bfloat16),
            pltpu.VMEM((2048, 512), f32),
            pltpu.VMEM((2048, 512), f32),
            pltpu.VMEM((512, 512), f32),
            pltpu.VMEM((1024, 1024), f32),
            pltpu.SemaphoreType.DMA((6,)),
        ],
        compiler_params=pltpu.CompilerParams(vmem_limit_bytes=60 * 1024 * 1024),
        name="finish",
    )(sum_w, sum_o, ng, far_ng, tokens, cot, small, mixed, vecs)


def on_device(
    tokens, segments, in_gain, w_in, conv_w, conv_b, dt_bias, a_log, d_skip, gate_gain, w_out,
    cotangent,
):
    bf16 = jnp.bfloat16
    grp = lax.axis_index("grp")
    heads = jnp.stack([dt_bias, a_log, d_skip]).astype(jnp.float32)
    heads = jnp.where(grp == 0, jnp.pad(heads, ((0, 0), (0, 112))), jnp.pad(heads, ((0, 0), (16, 96))))
    rows = [
        in_gain.reshape(4, 128),
        conv_w.reshape(36, 128),
        conv_b.reshape(9, 128),
        gate_gain.reshape(8, 128),
        heads,
    ]
    small, at = 0.0, 0
    for part in rows:
        count = part.shape[0]
        small = small + jnp.pad(part.astype(jnp.float32), ((at, 64 - at - count), (0, 0)))
        at += count
    small = small.astype(bf16)
    seg = jnp.broadcast_to(segments[None], (8, 256))
    w_held, small_all, seg_all, tok_all = gather(w_in, small, seg, tokens)
    branch, mixed, pg, ng, strip, normed, cot_all, vecs, *far = layer_grads(
        tok_all, seg_all, small_all, w_held, w_out, cotangent
    )
    vecs = lax.dynamic_index_in_dim(lax.psum(vecs, ("rep", "grp")), grp, 0, False)
    sum_w, sum_o, far_ng = reduce_gradients(normed, pg, branch, cot_all, strip, ng, far)
    w_in_t, w_out_grad, input_grad, mixed, gain, conv_w_grad, conv_b_grad, per_head, gate = finish(
        sum_w, sum_o, ng, far_ng, tokens, cotangent, small_all, mixed, vecs
    )
    return (
        mixed,
        input_grad,
        gain.reshape(512),
        w_in_t.T,
        conv_w_grad,
        conv_b_grad.reshape(1152),
        per_head[1, 0:16],
        per_head[2, 0:16],
        per_head[3, 0:16],
        gate.reshape(1024),
        w_out_grad,
    )


def solution(mesh):
    placed = (
        P(("rep", "grp"), None),
        P(("rep", "grp")),
        P("grp"),
        P("grp", None),
        P(None, "grp"),
        P("grp"),
        P("grp"),
        P("grp"),
        P("grp"),
        P("grp"),
        P("grp", None),
        P(("rep", "grp"), None),
    )
    return jax.shard_map(
        on_device,
        mesh=mesh,
        in_specs=placed,
        out_specs=(
            P(("rep", "grp"), None),
            P(("rep", "grp"), None),
            P("grp"),
            P("grp", None),
            P(None, "grp"),
            P("grp"),
            P("grp"),
            P("grp"),
            P("grp"),
            P("grp"),
            P("grp", None),
        ),
        check_vma=False,
    )
```
